256 devices in a mesh: pair: 64 (over y, x_hi, z), row: 4 (over x_lo, core).
Axes of the slice: x: 4 (x_hi: 2, x_lo: 2; x = x_hi * 2 + x_lo), y: 4, z: 8, core: 2. Of those that a mesh axis runs over, the one named last changes fastest.
Arguments:
- matrix: float32 [16384, 16384], P('row', 'pair')
- plan: int32 [2], replicated, may hold values from 1 to 63, as said below
Outputs:
- final_matrix: float32 [16384, 16384], P('row', 'pair')
The draws below stay inside these ranges and needn't reach their ends.
Inputs may be any that keep to these rules, and one draw needn't show every extreme that they name: Round r pairs pair index p with p XOR plan[r]; the 2 masks are distinct and one of them equals 63.
All inputs are finite; a program needn't handle non-finite values.
Results may differ from the reference program's by a relative error of at most 0.0003.
Values sent between devices are 32-bit elements; how exact they have to be, the bound alone decides.
A program may use at most 64 MiB of HBM per device.

```python
import jax
import jax.numpy as jnp
from jax import lax

BLOCK = 128
ROUNDS = 2
SETS = 16
ROWS = 16384
NCOLS = 16384
N_PAIR = 64


def draw_matrix(key, part):
    key = jax.random.fold_in(key, 7)
    noise_key, scale_key = jax.random.split(key, 2)
    column_scale = jnp.exp(jax.random.uniform(scale_key, (1, NCOLS), jnp.float32) * jnp.log(10.0)) * 0.3
    noise = jax.random.normal(noise_key, (ROWS, NCOLS), jnp.float32)
    values = noise * column_scale
    return values.astype(jnp.float32)


def draw_plan(key, part):
    key = jax.random.fold_in(key, 11)
    mask_key, order_key = jax.random.split(key, 2)
    others = jax.random.permutation(mask_key, N_PAIR - 2)[:ROUNDS - 1].astype(jnp.int32) + 1
    masks = jnp.concatenate([others, jnp.full((1,), N_PAIR - 1, jnp.int32)])
    order = jax.random.permutation(order_key, ROUNDS)
    return masks[order].astype(jnp.int32)


def setup_inputs(seed: int = 0) -> dict:
    streams_of = jax.random.split(jax.random.key(seed), 3)
    matrix = draw_matrix(jax.random.fold_in(streams_of[2], 71), 0)
    plan = draw_plan(jax.random.fold_in(streams_of[2], 71), 0)
    return {"matrix": matrix, "plan": plan}


def pairing(set_index, columns):
    position = jnp.arange(columns, dtype=jnp.int32)
    last_player = columns - 1
    phase = jnp.asarray(set_index).astype(jnp.int32) % last_player
    partner = (2 * phase - position) % last_player
    partner = jnp.where(partner == position, last_player, partner)
    partner = jnp.where(position == last_player, phase, partner)
    return (position, partner.astype(jnp.int32))

def jacobi_solve(gram_matrix):
    columns = gram_matrix.shape[0]

    def rotation_set(set_index, carry):
        current_gram, vectors = carry
        position, partner = pairing(set_index, columns)
        diagonal = jnp.diagonal(current_gram)
        lower_index = jnp.minimum(position, partner)
        upper_index = jnp.maximum(position, partner)
        first = diagonal[lower_index]
        second = diagonal[upper_index]
        coupling = current_gram[position, partner]
        difference = second - first
        direction = jnp.where(difference >= 0, 1.0, -1.0).astype(jnp.float32)
        tangent = 2.0 * coupling * direction / (jnp.abs(difference) + jnp.sqrt(difference * difference + 4.0 * coupling * coupling) + 1e-06 * (first + second))
        cosine = 1.0 / jnp.sqrt(1.0 + tangent * tangent)
        orient = jnp.where(position < partner, -1.0, 1.0).astype(jnp.float32)
        coupled = orient * cosine * tangent
        current_gram = current_gram * cosine[None, :] + current_gram[:, partner] * coupled[None, :]
        current_gram = current_gram * cosine[:, None] + current_gram[partner, :] * coupled[:, None]
        vectors = vectors * cosine[None, :] + vectors[:, partner] * coupled[None, :]
        return (current_gram, vectors)
    start = (gram_matrix, jnp.eye(columns, dtype=jnp.float32))
    return lax.fori_loop(0, SETS, rotation_set, start)[1]

def gram_of(current):
    return lax.dot_general(current, current, (((0,), (0,)), ((), ())), precision=lax.Precision.HIGHEST, preferred_element_type=jnp.float32)

def reference(matrix, plan):
    row_count = matrix.shape[0]
    pair_count = matrix.shape[1] // (2 * BLOCK)
    blocks = matrix.reshape(row_count, pair_count, 2 * BLOCK).transpose(1, 0, 2)

    def rotate_pair(current):
        vectors = jacobi_solve(gram_of(current))
        return jnp.dot(current, vectors, precision=lax.Precision.HIGHEST, preferred_element_type=jnp.float32)
    for round_index in range(ROUNDS):
        rotated = lax.map(rotate_pair, blocks)
        source = jnp.bitwise_xor(jnp.arange(pair_count, dtype=jnp.int32), plan[round_index].astype(jnp.int32))
        right_block = rotated[:, :, BLOCK:][source]
        blocks = jnp.concatenate([rotated[:, :, :BLOCK], right_block], axis=2)
    return blocks.transpose(1, 0, 2).reshape(row_count, pair_count * 2 * BLOCK)
```

```python
import functools
import jax
import jax.numpy as jnp
from jax import lax
from jax.experimental import pallas as pl
from jax.experimental.pallas import tpu as pltpu
from jax.sharding import PartitionSpec as P

F32 = jnp.float32
BF16 = jnp.bfloat16
B = 128
SETS = 16


def lanes(shape):
    return lax.broadcasted_iota(jnp.int32, shape, len(shape) - 1)


def lane_gather(x, index):
    return jnp.take_along_axis(x, jnp.broadcast_to(index, x.shape), axis=1, mode="promise_in_bounds")


def shift_lanes(top, bottom):
    lane = lanes(top.shape)
    new_top = jnp.where(lane == B - 1, bottom, pltpu.roll(top, B - 1, 1))
    new_bottom = jnp.where(lane == 0, bottom, pltpu.roll(jnp.where(lane == 0, top, bottom), 1, 1))
    return new_top, new_bottom


def angles(first, second, coupling, step):
    lane = lanes(first.shape)
    top_is_lower = (lane == 0) | (lane > step)
    difference = second - first
    forward = (difference > 0) | ((difference == 0) & top_is_lower)
    tangent = jnp.where(forward, 2.0, -2.0) * coupling / (
        jnp.abs(difference)
        + jnp.sqrt(difference * difference + 4.0 * coupling * coupling)
        + 1e-06 * (first + second)
    )
    cosine = 1.0 / jnp.sqrt(1.0 + tangent * tangent)
    return cosine, cosine * tangent


def one_set(step, p, grams, v_top, v_bot):
    tt, tb, bt, bb = grams
    q = 1 - p
    eye = lax.broadcasted_iota(jnp.int32, (B, B), 0) == lanes((B, B))
    diag = lambda ref, base: jnp.sum(jnp.where(eye, ref[p, base : base + B, :], 0.0), axis=0, keepdims=True)
    cosine, sine = angles(diag(tt, 1), diag(bb, 7), diag(tb, 1), step)
    col_c = jnp.broadcast_to(cosine, (B, B)).T
    col_s = jnp.broadcast_to(sine, (B, B)).T
    n = 32
    for k in range(0, B, n):
        a, b = tt[p, 1 + k : 1 + k + n, :], tb[p, 1 + k : 1 + k + n, :]
        c, d = bt[p, 7 + k : 7 + k + n, :], bb[p, 7 + k : 7 + k + n, :]
        a, b = cosine * a - sine * b, cosine * b + sine * a
        c, d = cosine * c - sine * d, cosine * d + sine * c
        cc, ss = col_c[k : k + n], col_s[k : k + n]
        a, c = cc * a - ss * c, cc * c + ss * a
        b, d = cc * b - ss * d, cc * d + ss * b
        a, b = shift_lanes(a, b)
        c, d = shift_lanes(c, d)
        tt[q, k : k + n, :], tb[q, k : k + n, :] = a, b
        bt[q, 8 + k : 8 + k + n, :], bb[q, 8 + k : 8 + k + n, :] = c, d
    for top, bottom in ((tt, bt), (tb, bb)):
        first = bottom[q, 8:9, :]
        top[q, B : B + 1, :] = bottom[q, B + 7 : B + 8, :]
        bottom[q, 7:8, :] = first
        bottom[q, 8:9, :] = top[q, 0:1, :]
    for k in range(0, 2 * B, n):
        a, b = v_top[k : k + n, :], v_bot[k : k + n, :]
        a, b = shift_lanes(cosine * a - sine * b, cosine * b + sine * a)
        v_top[k : k + n, :], v_bot[k : k + n, :] = a, b


def jacobi(ll, lr, rr, grams, v_top, v_bot):
    tt, tb, bt, bb = grams
    lane = lanes((1, B))
    lr = lane_gather(lr, B - 1 - lane)
    rr = lane_gather(lane_gather(rr, B - 1 - lane).T, B - 1 - lane)
    tt[0, 1 : B + 1, :] = ll
    tb[0, 1 : B + 1, :] = lr
    bt[0, 7 : B + 7, :] = lr.T
    bb[0, 7 : B + 7, :] = rr
    row = lax.broadcasted_iota(jnp.int32, (2 * B, B), 0)
    v_top[...] = jnp.where(row == lanes((2 * B, B)), 1.0, 0.0)
    v_bot[...] = jnp.where(row + lanes((2 * B, B)) == 2 * B - 1, 1.0, 0.0)

    @pl.loop(0, SETS // 2)
    def _(i):
        one_set(2 * i, 0, grams, v_top, v_bot)
        one_set(2 * i + 1, 1, grams, v_top, v_bot)

    top, bottom = v_top[...], v_bot[...]
    lane = lanes((1, B))
    moved = pltpu.roll(top, SETS, 1)
    low = lane < SETS
    left = jnp.where(low, lane_gather(bottom, (SETS - lane) & (B - 1)), moved)
    right = jnp.where(low, moved, lane_gather(bottom, jnp.where(lane == B - 1, 0, (B + SETS - 1 - lane) & (B - 1))))
    return left, right

ROWS = 4096
CHUNK = 512
CHUNKS = ROWS // CHUNK
MESH = pl.DeviceIdType.MESH


def split(x):
    high = x.astype(BF16)
    return high, (x - high.astype(F32)).astype(BF16)


def gram_blocks(y, products, squares, arrive):
    products[...] = jnp.zeros_like(products)
    squares[...] = jnp.zeros_like(squares)

    @pl.loop(0, CHUNKS)
    def _(i):
        arrive(i)
        x = y[pl.ds(i * CHUNK, CHUNK), :]
        high, low = split(x)
        products[...] += lax.dot_general(
            high, jnp.concatenate([high, low], axis=1), (((0,), (0,)), ((), ())), preferred_element_type=F32
        )
        small = low.astype(F32)
        squares[...] += jnp.sum((small * small).reshape(CHUNK // 8, 8, 2 * B), axis=0)

    eye = lax.broadcasted_iota(jnp.int32, (B, B), 0) == lanes((B, B))
    low_square = jnp.sum(squares[...], axis=0, keepdims=True)
    ll = products[:B, 2 * B : 3 * B]
    lr = products[:B, 3 * B :]
    rl = products[B:, 2 * B : 3 * B]
    rr = products[B:, 3 * B :]
    return (
        products[:B, :B] + (ll + ll.T) + jnp.where(eye, low_square[:, :B], 0.0),
        products[:B, B : 2 * B] + (lr + rl.T),
        products[B:, B : 2 * B] + (rr + rr.T) + jnp.where(eye, low_square[:, B:], 0.0),
    )


HALF = 3 * B // 2


def row_sum(part, recv_a, acc, recv_b, full, send, recv):
    pair, row = lax.axis_index("pair"), lax.axis_index("row")
    core, chip = lax.rem(row, 2), lax.div(row, 2)
    mate = (pair, 2 * chip + 1 - core)
    across = (pair, 2 * (1 - chip) + core)
    mine, other = pl.ds(core * HALF, HALF), pl.ds((1 - core) * HALF, HALF)

    def copy(k, src, dst, device):
        return pltpu.make_async_remote_copy(
            src_ref=src, dst_ref=dst, send_sem=send.at[k], recv_sem=recv.at[k], device_id=device, device_id_type=MESH
        )

    pl.semaphore_wait(pltpu.get_barrier_semaphore(), 2)
    first = copy(0, part.at[other, :], recv_a, mate)
    first.start()
    first.wait()
    acc[...] = part[mine, :] + recv_a[...]
    second = copy(1, acc, recv_b, across)
    second.start()
    second.wait()
    full[mine, :] = acc[...] + recv_b[...]
    third = copy(2, full.at[mine, :], full.at[mine, :], mate)
    third.start()
    third.wait()


def announce():
    pair, row = lax.axis_index("pair"), lax.axis_index("row")
    core, chip = lax.rem(row, 2), lax.div(row, 2)
    barrier = pltpu.get_barrier_semaphore()
    for device in ((pair, 2 * chip + 1 - core), (pair, 2 * (1 - chip) + core)):
        pl.semaphore_signal(barrier, inc=1, device_id=device, device_id_type=MESH)


def round_kernel(whole, *refs):
    ins, refs = (refs[:1], refs[1:]) if whole else (refs[:2], refs[2:])
    left_out, right_out, y, products, squares, part, recv_a, acc, recv_b, full, v_high, v_low = refs[:12]
    grams, (v_top, v_bot), (load, store, send, recv) = refs[12:16], refs[16:18], refs[18:]
    announce()

    def loads(i):
        rows = pl.ds(i * CHUNK, CHUNK)
        if whole:
            return [pltpu.make_async_copy(ins[0].at[rows, :], y.at[rows, :], load.at[i, 0])]
        return [
            pltpu.make_async_copy(ins[0].at[rows, :], y.at[rows, pl.ds(0, B)], load.at[i, 0]),
            pltpu.make_async_copy(ins[1].at[rows, :], y.at[rows, pl.ds(B, B)], load.at[i, 1]),
        ]

    def stores(i):
        rows = pl.ds(i * CHUNK, CHUNK)
        return [
            pltpu.make_async_copy(y.at[rows, pl.ds(0, B)], left_out.at[rows, pl.ds(0, B)], store.at[i, 0]),
            pltpu.make_async_copy(y.at[rows, pl.ds(B, B)], right_out.at[rows, :], store.at[i, 1]),
        ]

    for i in range(CHUNKS):
        for c in loads(i):
            c.start()

    def arrive(i):
        for c in loads(i):
            c.wait()

    part[:B, :], part[B : 2 * B, :], part[2 * B :, :] = gram_blocks(y, products, squares, arrive)
    row_sum(part, recv_a, acc, recv_b, full, send, recv)
    left, right = jacobi(full[:B, :], full[B : 2 * B, :], full[2 * B :, :], grams, v_top, v_bot)
    v_high[:, :B], v_low[:, :B] = split(left)
    v_high[:, B:], v_low[:, B:] = split(right)

    @pl.loop(0, CHUNKS)
    def _(i):
        rows = pl.ds(i * CHUNK, CHUNK)
        high, low = split(y[rows, :])
        dot = functools.partial(jnp.dot, preferred_element_type=F32)
        y[rows, :] = dot(high, v_high[...]) + (dot(high, v_low[...]) + dot(low, v_high[...]))
        for c in stores(i):
            c.start()

    @pl.loop(0, CHUNKS)
    def _(i):
        for c in stores(i):
            c.wait()


def one_round(index, ins, left_width):
    flops = 2 * ROWS * (2 * B) ** 2 * 5
    return pl.pallas_call(
        functools.partial(round_kernel, len(ins) == 1),
        out_shape=(jax.ShapeDtypeStruct((ROWS, left_width), F32), jax.ShapeDtypeStruct((ROWS, B), F32)),
        in_specs=[pl.BlockSpec(memory_space=pl.ANY)] * len(ins),
        out_specs=(pl.BlockSpec(memory_space=pl.ANY), pl.BlockSpec(memory_space=pl.ANY)),
        scratch_shapes=[
            pltpu.VMEM((ROWS, 2 * B), F32),
            pltpu.VMEM((2 * B, 4 * B), F32),
            pltpu.VMEM((8, 2 * B), F32),
            pltpu.VMEM((3 * B, B), F32),
            pltpu.VMEM((HALF, B), F32),
            pltpu.VMEM((HALF, B), F32),
            pltpu.VMEM((HALF, B), F32),
            pltpu.VMEM((3 * B, B), F32),
            pltpu.VMEM((2 * B, 2 * B), BF16),
            pltpu.VMEM((2 * B, 2 * B), BF16),
        ]
        + [pltpu.VMEM((2, B + 16, B), F32) for _ in range(4)]
        + [pltpu.VMEM((2 * B, B), F32) for _ in range(2)]
        + [
            pltpu.SemaphoreType.DMA((CHUNKS, 2)),
            pltpu.SemaphoreType.DMA((CHUNKS, 2)),
            pltpu.SemaphoreType.DMA((3,)),
            pltpu.SemaphoreType.DMA((3,)),
        ],
        compiler_params=pltpu.CompilerParams(
            collective_id=index, has_side_effects=True, vmem_limit_bytes=40 * 2**20
        ),
        cost_estimate=pl.CostEstimate(flops=flops, bytes_accessed=4 * ROWS * B * 4, transcendentals=0),
        name="round",
    )(*ins)


def place_kernel(_, block, out, sem):
    copies = []
    for i in range(CHUNKS):
        rows = pl.ds(i * CHUNK, CHUNK)
        copies.append(pltpu.make_async_copy(block.at[rows, :], out.at[rows, pl.ds(B, B)], sem.at[i]))
    for c in copies:
        c.start()
    for c in copies:
        c.wait()


def place_right(out, block):
    return pl.pallas_call(
        place_kernel,
        out_shape=jax.ShapeDtypeStruct(out.shape, F32),
        in_specs=[pl.BlockSpec(memory_space=pl.ANY)] * 2,
        out_specs=pl.BlockSpec(memory_space=pl.ANY),
        scratch_shapes=[pltpu.SemaphoreType.DMA((CHUNKS,))],
        input_output_aliases={0: 0},
        cost_estimate=pl.CostEstimate(flops=0, bytes_accessed=2 * ROWS * B * 4, transcendentals=0),
        name="place",
    )(out, block)


def send_to(mask, block):
    count = lax.axis_size("pair")
    return lax.ppermute(block, "pair", [(i, i ^ mask) for i in range(count)])


def route(block, mask):
    masks = range(1, lax.axis_size("pair"))
    return lax.switch(mask - 1, [functools.partial(send_to, m) for m in masks], block)


def local(matrix, plan):
    left, right = one_round(0, (matrix,), B)
    right = route(right, plan[0])
    out, right = one_round(1, (left, right), 2 * B)
    return place_right(out, route(right, plan[1]))


def solution(mesh):
    return jax.shard_map(
        local, mesh=mesh, in_specs=(P("row", "pair"), P()), out_specs=P("row", "pair"), check_vma=False
    )
```

```python
import functools
import jax
import jax.numpy as jnp
from jax import lax
from jax.experimental import pallas as pl
from jax.experimental.pallas import tpu as pltpu
from jax.sharding import PartitionSpec as P

F32 = jnp.float32
BF16 = jnp.bfloat16
B = 128
SETS = 16


def lanes(shape):
    return lax.broadcasted_iota(jnp.int32, shape, len(shape) - 1)


def lane_gather(x, index):
    return jnp.take_along_axis(x, jnp.broadcast_to(index, x.shape), axis=1, mode="promise_in_bounds")


def shift_lanes(top, bottom):
    lane = lanes(top.shape)
    new_top = jnp.where(lane == B - 1, bottom, pltpu.roll(top, B - 1, 1))
    new_bottom = jnp.where(lane == 0, bottom, pltpu.roll(jnp.where(lane == 0, top, bottom), 1, 1))
    return new_top, new_bottom


def angles(first, second, coupling, step):
    lane = lanes(first.shape)
    top_is_lower = (lane == 0) | (lane > step)
    difference = second - first
    forward = (difference > 0) | ((difference == 0) & top_is_lower)
    tangent = jnp.where(forward, 2.0, -2.0) * coupling / (
        jnp.abs(difference)
        + jnp.sqrt(difference * difference + 4.0 * coupling * coupling)
        + 1e-06 * (first + second)
    )
    cosine = 1.0 / jnp.sqrt(1.0 + tangent * tangent)
    return cosine, cosine * tangent


def one_set(step, p, grams, v_top, v_bot):
    tt, tb, bt, bb = grams
    q = 1 - p
    eye = lax.broadcasted_iota(jnp.int32, (B, B), 0) == lanes((B, B))
    diag = lambda ref, base: jnp.sum(jnp.where(eye, ref[p, base : base + B, :], 0.0), axis=0, keepdims=True)
    cosine, sine = angles(diag(tt, 1), diag(bb, 7), diag(tb, 1), step)
    col_c = jnp.broadcast_to(cosine, (B, B)).T
    col_s = jnp.broadcast_to(sine, (B, B)).T
    n = 32
    for k in range(0, B, n):
        a, b = tt[p, 1 + k : 1 + k + n, :], tb[p, 1 + k : 1 + k + n, :]
        c, d = bt[p, 7 + k : 7 + k + n, :], bb[p, 7 + k : 7 + k + n, :]
        a, b = cosine * a - sine * b, cosine * b + sine * a
        c, d = cosine * c - sine * d, cosine * d + sine * c
        cc, ss = col_c[k : k + n], col_s[k : k + n]
        a, c = cc * a - ss * c, cc * c + ss * a
        b, d = cc * b - ss * d, cc * d + ss * b
        a, b = shift_lanes(a, b)
        c, d = shift_lanes(c, d)
        tt[q, k : k + n, :], tb[q, k : k + n, :] = a, b
        bt[q, 8 + k : 8 + k + n, :], bb[q, 8 + k : 8 + k + n, :] = c, d
    for top, bottom in ((tt, bt), (tb, bb)):
        first = bottom[q, 8:9, :]
        top[q, B : B + 1, :] = bottom[q, B + 7 : B + 8, :]
        bottom[q, 7:8, :] = first
        bottom[q, 8:9, :] = top[q, 0:1, :]
    for k in range(0, 2 * B, n):
        a, b = v_top[k : k + n, :], v_bot[k : k + n, :]
        a, b = shift_lanes(cosine * a - sine * b, cosine * b + sine * a)
        v_top[k : k + n, :], v_bot[k : k + n, :] = a, b


def jacobi(ll, lr, rr, grams, v_top, v_bot):
    tt, tb, bt, bb = grams
    lane = lanes((1, B))
    lr = lane_gather(lr, B - 1 - lane)
    rr = lane_gather(lane_gather(rr, B - 1 - lane).T, B - 1 - lane)
    tt[0, 1 : B + 1, :] = ll
    tb[0, 1 : B + 1, :] = lr
    bt[0, 7 : B + 7, :] = lr.T
    bb[0, 7 : B + 7, :] = rr
    row = lax.broadcasted_iota(jnp.int32, (2 * B, B), 0)
    v_top[...] = jnp.where(row == lanes((2 * B, B)), 1.0, 0.0)
    v_bot[...] = jnp.where(row + lanes((2 * B, B)) == 2 * B - 1, 1.0, 0.0)

    @pl.loop(0, SETS // 2)
    def _(i):
        one_set(2 * i, 0, grams, v_top, v_bot)
        one_set(2 * i + 1, 1, grams, v_top, v_bot)

    top, bottom = v_top[...], v_bot[...]
    lane = lanes((1, B))
    moved = pltpu.roll(top, SETS, 1)
    low = lane < SETS
    left = jnp.where(low, lane_gather(bottom, (SETS - lane) & (B - 1)), moved)
    right = jnp.where(low, moved, lane_gather(bottom, jnp.where(lane == B - 1, 0, (B + SETS - 1 - lane) & (B - 1))))
    return left, right

ROWS = 4096
CHUNK = 512
CHUNKS = ROWS // CHUNK
MESH = pl.DeviceIdType.MESH


def split(x):
    high = x.astype(BF16)
    return high, (x - high.astype(F32)).astype(BF16)


def gram_blocks(y, products, squares, arrive):
    products[...] = jnp.zeros_like(products)
    squares[...] = jnp.zeros_like(squares)

    @pl.loop(0, CHUNKS)
    def _(i):
        arrive(i)
        x = y[pl.ds(i * CHUNK, CHUNK), :]
        high, low = split(x)
        products[...] += lax.dot_general(
            high, jnp.concatenate([high, low], axis=1), (((0,), (0,)), ((), ())), preferred_element_type=F32
        )
        small = low.astype(F32)
        squares[...] += jnp.sum((small * small).reshape(CHUNK // 8, 8, 2 * B), axis=0)

    eye = lax.broadcasted_iota(jnp.int32, (B, B), 0) == lanes((B, B))
    low_square = jnp.sum(squares[...], axis=0, keepdims=True)
    ll = products[:B, 2 * B : 3 * B]
    lr = products[:B, 3 * B :]
    rl = products[B:, 2 * B : 3 * B]
    rr = products[B:, 3 * B :]
    return (
        products[:B, :B] + (ll + ll.T) + jnp.where(eye, low_square[:, :B], 0.0),
        products[:B, B : 2 * B] + (lr + rl.T),
        products[B:, B : 2 * B] + (rr + rr.T) + jnp.where(eye, low_square[:, B:], 0.0),
    )


HALF = 3 * B // 2


def row_sum(part, recv_a, acc, recv_b, full, send, recv):
    pair, row = lax.axis_index("pair"), lax.axis_index("row")
    core, chip = lax.rem(row, 2), lax.div(row, 2)
    mate = (pair, 2 * chip + 1 - core)
    across = (pair, 2 * (1 - chip) + core)
    mine, other = pl.ds(core * HALF, HALF), pl.ds((1 - core) * HALF, HALF)

    def copy(k, src, dst, device):
        return pltpu.make_async_remote_copy(
            src_ref=src, dst_ref=dst, send_sem=send.at[k], recv_sem=recv.at[k], device_id=device, device_id_type=MESH
        )

    pl.semaphore_wait(pltpu.get_barrier_semaphore(), 2)
    first = copy(0, part.at[other, :], recv_a, mate)
    first.start()
    first.wait()
    acc[...] = part[mine, :] + recv_a[...]
    second = copy(1, acc, recv_b, across)
    second.start()
    second.wait()
    full[mine, :] = acc[...] + recv_b[...]
    third = copy(2, full.at[mine, :], full.at[mine, :], mate)
    third.start()
    third.wait()


def announce():
    pair, row = lax.axis_index("pair"), lax.axis_index("row")
    core, chip = lax.rem(row, 2), lax.div(row, 2)
    barrier = pltpu.get_barrier_semaphore()
    for device in ((pair, 2 * chip + 1 - core), (pair, 2 * (1 - chip) + core)):
        pl.semaphore_signal(barrier, inc=1, device_id=device, device_id_type=MESH)


def round_kernel(whole, *refs):
    ins, refs = (refs[:1], refs[1:]) if whole else (refs[:2], refs[2:])
    left_out, right_out, y, products, squares, part, recv_a, acc, recv_b, full, v_high, v_low = refs[:12]
    grams, (v_top, v_bot), (load, store, send, recv) = refs[12:16], refs[16:18], refs[18:]
    announce()

    def loads(i):
        rows = pl.ds(i * CHUNK, CHUNK)
        if whole:
            return [pltpu.make_async_copy(ins[0].at[rows, :], y.at[rows, :], load.at[i, 0])]
        return [
            pltpu.make_async_copy(ins[0].at[rows, :], y.at[rows, pl.ds(0, B)], load.at[i, 0]),
            pltpu.make_async_copy(ins[1].at[rows, :], y.at[rows, pl.ds(B, B)], load.at[i, 1]),
        ]

    def stores(i):
        rows = pl.ds(i * CHUNK, CHUNK)
        return [
            pltpu.make_async_copy(y.at[rows, pl.ds(0, B)], left_out.at[rows, :], store.at[i, 0]),
            pltpu.make_async_copy(y.at[rows, pl.ds(B, B)], right_out.at[rows, :], store.at[i, 1]),
        ]

    for i in range(CHUNKS):
        for c in loads(i):
            c.start()

    def arrive(i):
        for c in loads(i):
            c.wait()

    part[:B, :], part[B : 2 * B, :], part[2 * B :, :] = gram_blocks(y, products, squares, arrive)
    row_sum(part, recv_a, acc, recv_b, full, send, recv)
    left, right = jacobi(full[:B, :], full[B : 2 * B, :], full[2 * B :, :], grams, v_top, v_bot)
    v_high[:, :B], v_low[:, :B] = split(left)
    v_high[:, B:], v_low[:, B:] = split(right)

    @pl.loop(0, CHUNKS)
    def _(i):
        rows = pl.ds(i * CHUNK, CHUNK)
        high, low = split(y[rows, :])
        dot = functools.partial(jnp.dot, preferred_element_type=F32)
        y[rows, :] = dot(high, v_high[...]) + (dot(high, v_low[...]) + dot(low, v_high[...]))
        for c in stores(i):
            c.start()

    @pl.loop(0, CHUNKS)
    def _(i):
        for c in stores(i):
            c.wait()


def one_round(index, ins):
    flops = 2 * ROWS * (2 * B) ** 2 * 5
    return pl.pallas_call(
        functools.partial(round_kernel, len(ins) == 1),
        out_shape=(jax.ShapeDtypeStruct((ROWS, B), F32),) * 2,
        in_specs=[pl.BlockSpec(memory_space=pl.ANY)] * len(ins),
        out_specs=(pl.BlockSpec(memory_space=pl.ANY), pl.BlockSpec(memory_space=pl.ANY)),
        scratch_shapes=[
            pltpu.VMEM((ROWS, 2 * B), F32),
            pltpu.VMEM((2 * B, 4 * B), F32),
            pltpu.VMEM((8, 2 * B), F32),
            pltpu.VMEM((3 * B, B), F32),
            pltpu.VMEM((HALF, B), F32),
            pltpu.VMEM((HALF, B), F32),
            pltpu.VMEM((HALF, B), F32),
            pltpu.VMEM((3 * B, B), F32),
            pltpu.VMEM((2 * B, 2 * B), BF16),
            pltpu.VMEM((2 * B, 2 * B), BF16),
        ]
        + [pltpu.VMEM((2, B + 16, B), F32) for _ in range(4)]
        + [pltpu.VMEM((2 * B, B), F32) for _ in range(2)]
        + [
            pltpu.SemaphoreType.DMA((CHUNKS, 2)),
            pltpu.SemaphoreType.DMA((CHUNKS, 2)),
            pltpu.SemaphoreType.DMA((3,)),
            pltpu.SemaphoreType.DMA((3,)),
        ],
        compiler_params=pltpu.CompilerParams(
            collective_id=index, has_side_effects=True, vmem_limit_bytes=40 * 2**20
        ),
        cost_estimate=pl.CostEstimate(flops=flops, bytes_accessed=4 * ROWS * B * 4, transcendentals=0),
        name="round",
    )(*ins)


PARTS = 4


def transfer_kernel(mask, block, out, send, recv):
    to = (jnp.bitwise_xor(lax.axis_index("pair"), mask), lax.axis_index("row"))
    barrier = pltpu.get_barrier_semaphore()
    pl.semaphore_signal(barrier, inc=1, device_id=to, device_id_type=MESH)
    pl.semaphore_wait(barrier, 1)
    copies = []
    for i in range(PARTS):
        rows = pl.ds(i * (ROWS // PARTS), ROWS // PARTS)
        copies.append(
            pltpu.make_async_remote_copy(
                src_ref=block.at[rows, :],
                dst_ref=out.at[rows, :],
                send_sem=send.at[i],
                recv_sem=recv.at[i],
                device_id=to,
                device_id_type=MESH,
            )
        )
    for c in copies:
        c.start()
    for c in copies:
        c.wait()


def transfer(mask, block):
    if mask == 0:
        return block
    return pl.pallas_call(
        functools.partial(transfer_kernel, mask),
        out_shape=jax.ShapeDtypeStruct(block.shape, block.dtype),
        in_specs=[pl.BlockSpec(memory_space=pl.ANY)],
        out_specs=pl.BlockSpec(memory_space=pl.ANY),
        scratch_shapes=[pltpu.SemaphoreType.DMA((PARTS,)), pltpu.SemaphoreType.DMA((PARTS,))],
        compiler_params=pltpu.CompilerParams(collective_id=mask, has_side_effects=True),
        cost_estimate=pl.CostEstimate(flops=0, bytes_accessed=2 * ROWS * B * 4, transcendentals=0),
        name="transfer",
    )(block)


LOW_BITS = 3


def route(block, mask):
    count = lax.axis_size("pair")
    low_count = 1 << LOW_BITS

    def high_part(high, block):
        return lax.switch(
            jnp.bitwise_and(mask, low_count - 1),
            [functools.partial(transfer, high * low_count + low) for low in range(low_count)],
            block,
        )

    return lax.switch(
        jnp.right_shift(mask, LOW_BITS), [functools.partial(high_part, h) for h in range(count // low_count)], block
    )


def local(matrix, plan):
    left, right = one_round(64, (matrix,))
    right = route(right, plan[0])
    left, right = one_round(65, (left, right))
    return jnp.concatenate([left, route(right, plan[1])], axis=1)


def solution(mesh):
    return jax.shard_map(
        local, mesh=mesh, in_specs=(P("row", "pair"), P()), out_specs=P("row", "pair"), check_vma=False
    )
```

```python
import functools
import jax
import jax.numpy as jnp
from jax import lax
from jax.experimental import pallas as pl
from jax.experimental.pallas import tpu as pltpu
from jax.sharding import PartitionSpec as P

F32 = jnp.float32
BF16 = jnp.bfloat16
B = 128
SETS = 16


def lanes(shape):
    return lax.broadcasted_iota(jnp.int32, shape, len(shape) - 1)


def lane_gather(x, index):
    return jnp.take_along_axis(x, jnp.broadcast_to(index, x.shape), axis=1, mode="promise_in_bounds")


def shift_lanes(top, bottom):
    lane = lanes(top.shape)
    new_top = jnp.where(lane == B - 1, bottom, pltpu.roll(top, B - 1, 1))
    new_bottom = jnp.where(lane == 0, bottom, pltpu.roll(jnp.where(lane == 0, top, bottom), 1, 1))
    return new_top, new_bottom


def angles(first, second, coupling, step):
    lane = lanes(first.shape)
    top_is_lower = (lane == 0) | (lane > step)
    difference = second - first
    forward = (difference > 0) | ((difference == 0) & top_is_lower)
    tangent = jnp.where(forward, 2.0, -2.0) * coupling / (
        jnp.abs(difference)
        + jnp.sqrt(difference * difference + 4.0 * coupling * coupling)
        + 1e-06 * (first + second)
    )
    square = 1.0 + tangent * tangent
    cosine = 1.0 / jnp.sqrt(square)
    cosine += 0.5 * cosine * (1.0 - square * cosine * cosine)
    return cosine, cosine * tangent


def one_set(step, p, grams, v_top, v_bot):
    tt, tb, bt, bb = grams
    q = 1 - p
    eye = lax.broadcasted_iota(jnp.int32, (B, B), 0) == lanes((B, B))
    diag = lambda ref, base: jnp.sum(jnp.where(eye, ref[p, base : base + B, :], 0.0), axis=0, keepdims=True)
    cosine, sine = angles(diag(tt, 1), diag(bb, 7), diag(tb, 1), step)
    col_c = jnp.broadcast_to(cosine, (B, B)).T
    col_s = jnp.broadcast_to(sine, (B, B)).T
    n = 32
    for k in range(0, B, n):
        a, b = tt[p, 1 + k : 1 + k + n, :], tb[p, 1 + k : 1 + k + n, :]
        c, d = bt[p, 7 + k : 7 + k + n, :], bb[p, 7 + k : 7 + k + n, :]
        a, b = cosine * a - sine * b, cosine * b + sine * a
        c, d = cosine * c - sine * d, cosine * d + sine * c
        cc, ss = col_c[k : k + n], col_s[k : k + n]
        a, c = cc * a - ss * c, cc * c + ss * a
        b, d = cc * b - ss * d, cc * d + ss * b
        a, b = shift_lanes(a, b)
        c, d = shift_lanes(c, d)
        tt[q, k : k + n, :], tb[q, k : k + n, :] = a, b
        bt[q, 8 + k : 8 + k + n, :], bb[q, 8 + k : 8 + k + n, :] = c, d
    for top, bottom in ((tt, bt), (tb, bb)):
        first = bottom[q, 8:9, :]
        top[q, B : B + 1, :] = bottom[q, B + 7 : B + 8, :]
        bottom[q, 7:8, :] = first
        bottom[q, 8:9, :] = top[q, 0:1, :]
    for k in range(0, 2 * B, n):
        a, b = v_top[k : k + n, :], v_bot[k : k + n, :]
        a, b = shift_lanes(cosine * a - sine * b, cosine * b + sine * a)
        v_top[k : k + n, :], v_bot[k : k + n, :] = a, b


def jacobi(ll, lr, rr, grams, v_top, v_bot):
    tt, tb, bt, bb = grams
    lane = lanes((1, B))
    lr = lane_gather(lr, B - 1 - lane)
    rr = lane_gather(lane_gather(rr, B - 1 - lane).T, B - 1 - lane)
    tt[0, 1 : B + 1, :] = ll
    tb[0, 1 : B + 1, :] = lr
    bt[0, 7 : B + 7, :] = lr.T
    bb[0, 7 : B + 7, :] = rr
    row = lax.broadcasted_iota(jnp.int32, (2 * B, B), 0)
    v_top[...] = jnp.where(row == lanes((2 * B, B)), 1.0, 0.0)
    v_bot[...] = jnp.where(row + lanes((2 * B, B)) == 2 * B - 1, 1.0, 0.0)

    @pl.loop(0, SETS // 2)
    def _(i):
        one_set(2 * i, 0, grams, v_top, v_bot)
        one_set(2 * i + 1, 1, grams, v_top, v_bot)

    top, bottom = v_top[...], v_bot[...]
    lane = lanes((1, B))
    moved = pltpu.roll(top, SETS, 1)
    low = lane < SETS
    left = jnp.where(low, lane_gather(bottom, (SETS - lane) & (B - 1)), moved)
    right = jnp.where(low, moved, lane_gather(bottom, jnp.where(lane == B - 1, 0, (B + SETS - 1 - lane) & (B - 1))))
    return left, right


JACOBI_SCRATCH = [pltpu.VMEM((2, B + 16, B), F32) for _ in range(4)] + [pltpu.VMEM((2 * B, B), F32) for _ in range(2)]

ROWS = 4096
CHUNK = 512
CHUNKS = ROWS // CHUNK
MESH = pl.DeviceIdType.MESH
HBM = pl.BlockSpec(memory_space=pl.ANY)
WHOLE = pl.BlockSpec(memory_space=pltpu.VMEM)


def chunk(i):
    return pl.ds(pl.multiple_of(i * CHUNK, CHUNK), CHUNK)


def split(x):
    high = x.astype(BF16)
    return high, (x - high.astype(F32)).astype(BF16)


GRAM_SCRATCH = [pltpu.VMEM((2 * B, 4 * B), F32), pltpu.VMEM((8, 2 * B), F32)]


def gram_clear(products, squares):
    products[...] = jnp.zeros_like(products)
    squares[...] = jnp.zeros_like(squares)


def gram_add(x, products, squares):
    high, low = split(x)
    products[...] += lax.dot_general(
        high, jnp.concatenate([high, low], axis=1), (((0,), (0,)), ((), ())), preferred_element_type=F32
    )
    small = low.astype(F32)
    squares[...] += jnp.sum((small * small).reshape(x.shape[0] // 8, 8, 2 * B), axis=0)


def gram_blocks(products, squares, part):
    eye = lax.broadcasted_iota(jnp.int32, (B, B), 0) == lanes((B, B))
    low_square = jnp.sum(squares[...], axis=0, keepdims=True)
    ll = products[:B, 2 * B : 3 * B]
    lr = products[:B, 3 * B :]
    rl = products[B:, 2 * B : 3 * B]
    rr = products[B:, 3 * B :]
    part[:B, :] = products[:B, :B] + (ll + ll.T) + jnp.where(eye, low_square[:, :B], 0.0)
    part[B : 2 * B, :] = products[:B, B : 2 * B] + (lr + rl.T)
    part[2 * B :, :] = products[B:, B : 2 * B] + (rr + rr.T) + jnp.where(eye, low_square[:, B:], 0.0)


HALF = 3 * B // 2
SUM_SCRATCH = [
    pltpu.VMEM((HALF, B), F32),
    pltpu.VMEM((HALF, B), F32),
    pltpu.VMEM((HALF, B), F32),
    pltpu.VMEM((3 * B, B), F32),
    pltpu.SemaphoreType.DMA((3,)),
    pltpu.SemaphoreType.DMA((3,)),
]


def row_neighbours():
    pair, row = lax.axis_index("pair"), lax.axis_index("row")
    core, chip = lax.rem(row, 2), lax.div(row, 2)
    return core, (pair, 2 * chip + 1 - core), (pair, 2 * (1 - chip) + core)


def greet(devices):
    for device in devices:
        pl.semaphore_signal(pltpu.get_barrier_semaphore(), inc=1, device_id=device, device_id_type=MESH)


def remote(src, dst, send, recv, device):
    return pltpu.make_async_remote_copy(
        src_ref=src, dst_ref=dst, send_sem=send, recv_sem=recv, device_id=device, device_id_type=MESH
    )


def row_sum(part, recv_a, acc, recv_b, full, send, recv):
    core, mate, across = row_neighbours()
    mine, other = pl.ds(core * HALF, HALF), pl.ds((1 - core) * HALF, HALF)
    pl.semaphore_wait(pltpu.get_barrier_semaphore(), 2)
    first = remote(part.at[other, :], recv_a, send.at[0], recv.at[0], mate)
    first.start()
    first.wait()
    acc[...] = part[mine, :] + recv_a[...]
    second = remote(acc, recv_b, send.at[1], recv.at[1], across)
    second.start()
    second.wait()
    full[mine, :] = acc[...] + recv_b[...]
    third = remote(full.at[mine, :], full.at[mine, :], send.at[2], recv.at[2], mate)
    third.start()
    third.wait()


def round_kernel(count, *refs):
    ins, refs = refs[:count], refs[count:]
    left_out, right_out, x, v_high, v_low, load, store, part = refs[:8]
    gram, sums, solve = refs[8:10], refs[10:16], refs[16:]
    core, mate, across = row_neighbours()
    greet((mate, across))

    def loads(i):
        if count == 1:
            return [pltpu.make_async_copy(ins[0].at[chunk(i), :], x.at[chunk(i), :], load.at[i, 0])]
        return [
            pltpu.make_async_copy(ins[j].at[chunk(i), :], x.at[chunk(i), pl.ds(j * B, B)], load.at[i, j])
            for j in range(2)
        ]

    def stores(i):
        return [
            pltpu.make_async_copy(x.at[chunk(i), pl.ds(j * B, B)], out.at[chunk(i), :], store.at[i, j])
            for j, out in enumerate((left_out, right_out))
        ]

    @pl.loop(0, CHUNKS)
    def _(i):
        for c in loads(i):
            c.start()

    gram_clear(*gram)

    @pl.loop(0, CHUNKS)
    def _(i):
        for c in loads(i):
            c.wait()
        gram_add(x[chunk(i), :], *gram)

    gram_blocks(*gram, part)
    row_sum(part, *sums)
    full = sums[3]
    halves = jacobi(full[:B, :], full[B : 2 * B, :], full[2 * B :, :], solve[:4], *solve[4:])
    for j, half in enumerate(halves):
        v_high[:, j * B : (j + 1) * B], v_low[:, j * B : (j + 1) * B] = split(half)
    dot = functools.partial(jnp.dot, preferred_element_type=F32)

    @pl.loop(0, CHUNKS)
    def _(i):
        high, low = split(x[chunk(i), :])
        x[chunk(i), :] = dot(high, v_high[...]) + (dot(high, v_low[...]) + dot(low, v_high[...]))
        for c in stores(i):
            c.start()

    @pl.loop(0, CHUNKS)
    def _(i):
        for c in stores(i):
            c.wait()


def one_round(index, *ins):
    return pl.pallas_call(
        functools.partial(round_kernel, len(ins)),
        out_shape=(jax.ShapeDtypeStruct((ROWS, B), F32),) * 2,
        in_specs=[HBM] * len(ins),
        out_specs=(HBM, HBM),
        scratch_shapes=[
            pltpu.VMEM((ROWS, 2 * B), F32),
            pltpu.VMEM((2 * B, 2 * B), BF16),
            pltpu.VMEM((2 * B, 2 * B), BF16),
            pltpu.SemaphoreType.DMA((CHUNKS, 2)),
            pltpu.SemaphoreType.DMA((CHUNKS, 2)),
            pltpu.VMEM((3 * B, B), F32),
        ]
        + GRAM_SCRATCH
        + SUM_SCRATCH
        + JACOBI_SCRATCH,
        compiler_params=pltpu.CompilerParams(
            collective_id=index, has_side_effects=True, vmem_limit_bytes=VMEM_LIMIT
        ),
        cost_estimate=pl.CostEstimate(
            flops=10 * ROWS * (2 * B) ** 2, bytes_accessed=4 * ROWS * 2 * B * 2, transcendentals=0
        ),
        name="round",
    )(*ins)


LOW_BITS = 3
VMEM_LIMIT = 60 * 2**20


def transfer_kernel(mask, block, out, send, recv):
    to = (jnp.bitwise_xor(lax.axis_index("pair"), mask), lax.axis_index("row"))
    greet((to,))
    pl.semaphore_wait(pltpu.get_barrier_semaphore(), 1)
    copy = remote(block, out, send, recv, to)
    copy.start()
    copy.wait()


def transfer(mask, block):
    if mask == 0:
        return block
    return pl.pallas_call(
        functools.partial(transfer_kernel, mask),
        out_shape=jax.ShapeDtypeStruct(block.shape, block.dtype),
        in_specs=[HBM],
        out_specs=HBM,
        scratch_shapes=[pltpu.SemaphoreType.DMA, pltpu.SemaphoreType.DMA],
        compiler_params=pltpu.CompilerParams(collective_id=transfer_id(mask), has_side_effects=True),
        cost_estimate=pl.CostEstimate(flops=0, bytes_accessed=2 * ROWS * B * 4, transcendentals=0),
        name="transfer",
    )(block)


def transfer_id(mask):
    return 2 if mask == lax.axis_size("pair") - 1 else mask + 2


def route(block, mask):
    count = lax.axis_size("pair")
    low_count = 1 << LOW_BITS

    def high_part(high, block):
        return lax.switch(
            jnp.bitwise_and(mask, low_count - 1),
            [functools.partial(transfer, high * low_count + low) for low in range(low_count)],
            block,
        )

    return lax.switch(
        jnp.right_shift(mask, LOW_BITS), [functools.partial(high_part, h) for h in range(count // low_count)], block
    )


def local(matrix, plan):
    left, right = one_round(1, matrix[:, :B], matrix[:, B:])
    right = route(right, plan[0])
    left, right = one_round(1, left, right)
    return jnp.concatenate([left, route(right, plan[1])], axis=1)


def solution(mesh):
    return jax.shard_map(
        local, mesh=mesh, in_specs=(P("row", "pair"), P()), out_specs=P("row", "pair"), check_vma=False
    )
```

```python
import functools
import jax
import jax.numpy as jnp
from jax import lax
from jax.experimental import pallas as pl
from jax.experimental.pallas import tpu as pltpu
from jax.sharding import PartitionSpec as P

F32 = jnp.float32
BF16 = jnp.bfloat16
B = 128
SETS = 16


def lanes(shape):
    return lax.broadcasted_iota(jnp.int32, shape, len(shape) - 1)


def lane_gather(x, index):
    return jnp.take_along_axis(x, jnp.broadcast_to(index, x.shape), axis=1, mode="promise_in_bounds")


def shift_lanes(top, bottom):
    lane = lanes(top.shape)
    new_top = jnp.where(lane == B - 1, bottom, pltpu.roll(top, B - 1, 1))
    new_bottom = jnp.where(lane == 0, bottom, pltpu.roll(jnp.where(lane == 0, top, bottom), 1, 1))
    return new_top, new_bottom


def angles(first, second, coupling, step):
    lane = lanes(first.shape)
    top_is_lower = (lane == 0) | (lane > step)
    difference = second - first
    forward = (difference > 0) | ((difference == 0) & top_is_lower)
    tangent = jnp.where(forward, 2.0, -2.0) * coupling / (
        jnp.abs(difference)
        + jnp.sqrt(difference * difference + 4.0 * coupling * coupling)
        + 1e-06 * (first + second)
    )
    square = 1.0 + tangent * tangent
    cosine = 1.0 / jnp.sqrt(square)
    cosine += 0.5 * cosine * (1.0 - square * cosine * cosine)
    return cosine, cosine * tangent


def one_set(step, p, grams, v_top, v_bot):
    tt, tb, bt, bb = grams
    q = 1 - p
    eye = lax.broadcasted_iota(jnp.int32, (B, B), 0) == lanes((B, B))
    diag = lambda ref, base: jnp.sum(jnp.where(eye, ref[p, base : base + B, :], 0.0), axis=0, keepdims=True)
    cosine, sine = angles(diag(tt, 1), diag(bb, 7), diag(tb, 1), step)
    col_c = jnp.broadcast_to(cosine, (B, B)).T
    col_s = jnp.broadcast_to(sine, (B, B)).T
    n = 32
    for k in range(0, B, n):
        a, b = tt[p, 1 + k : 1 + k + n, :], tb[p, 1 + k : 1 + k + n, :]
        c, d = bt[p, 7 + k : 7 + k + n, :], bb[p, 7 + k : 7 + k + n, :]
        a, b = cosine * a - sine * b, cosine * b + sine * a
        c, d = cosine * c - sine * d, cosine * d + sine * c
        cc, ss = col_c[k : k + n], col_s[k : k + n]
        a, c = cc * a - ss * c, cc * c + ss * a
        b, d = cc * b - ss * d, cc * d + ss * b
        a, b = shift_lanes(a, b)
        c, d = shift_lanes(c, d)
        tt[q, k : k + n, :], tb[q, k : k + n, :] = a, b
        bt[q, 8 + k : 8 + k + n, :], bb[q, 8 + k : 8 + k + n, :] = c, d
    for top, bottom in ((tt, bt), (tb, bb)):
        first = bottom[q, 8:9, :]
        top[q, B : B + 1, :] = bottom[q, B + 7 : B + 8, :]
        bottom[q, 7:8, :] = first
        bottom[q, 8:9, :] = top[q, 0:1, :]
    for k in range(0, 2 * B, n):
        a, b = v_top[k : k + n, :], v_bot[k : k + n, :]
        a, b = shift_lanes(cosine * a - sine * b, cosine * b + sine * a)
        v_top[k : k + n, :], v_bot[k : k + n, :] = a, b


def jacobi(ll, lr, rr, grams, v_top, v_bot):
    tt, tb, bt, bb = grams
    lane = lanes((1, B))
    lr = lane_gather(lr, B - 1 - lane)
    rr = lane_gather(lane_gather(rr, B - 1 - lane).T, B - 1 - lane)
    tt[0, 1 : B + 1, :] = ll
    tb[0, 1 : B + 1, :] = lr
    bt[0, 7 : B + 7, :] = lr.T
    bb[0, 7 : B + 7, :] = rr
    row = lax.broadcasted_iota(jnp.int32, (2 * B, B), 0)
    v_top[...] = jnp.where(row == lanes((2 * B, B)), 1.0, 0.0)
    v_bot[...] = jnp.where(row + lanes((2 * B, B)) == 2 * B - 1, 1.0, 0.0)

    @pl.loop(0, SETS // 2)
    def _(i):
        one_set(2 * i, 0, grams, v_top, v_bot)
        one_set(2 * i + 1, 1, grams, v_top, v_bot)

    top, bottom = v_top[...], v_bot[...]
    lane = lanes((1, B))
    moved = pltpu.roll(top, SETS, 1)
    low = lane < SETS
    left = jnp.where(low, lane_gather(bottom, (SETS - lane) & (B - 1)), moved)
    right = jnp.where(low, moved, lane_gather(bottom, jnp.where(lane == B - 1, 0, (B + SETS - 1 - lane) & (B - 1))))
    return left, right


JACOBI_SCRATCH = [pltpu.VMEM((2, B + 16, B), F32) for _ in range(4)] + [pltpu.VMEM((2 * B, B), F32) for _ in range(2)]

ROWS = 4096
CHUNK = 512
CHUNKS = ROWS // CHUNK
MESH = pl.DeviceIdType.MESH
HBM = pl.BlockSpec(memory_space=pl.ANY)
WHOLE = pl.BlockSpec(memory_space=pltpu.VMEM)


def chunk(i):
    return pl.ds(pl.multiple_of(i * CHUNK, CHUNK), CHUNK)


def split(x):
    high = x.astype(BF16)
    return high, (x - high.astype(F32)).astype(BF16)


GRAM_SCRATCH = [pltpu.VMEM((2 * B, 6 * B), F32)]


def gram_clear(products):
    products[...] = jnp.zeros_like(products)


def gram_add(x, products):
    high = x.astype(BF16)
    rest = x - high.astype(F32)
    middle, low = split(rest)
    product = functools.partial(
        lax.dot_general, dimension_numbers=(((0,), (0,)), ((), ())), preferred_element_type=F32
    )
    products[:, : 4 * B] += product(high, jnp.concatenate([high, middle], axis=1))
    products[:, 2 * B : 4 * B] += product(high, low)
    products[:, 4 * B :] += product(middle, middle)


def gram_blocks(products, part):
    whole = products[:, : 2 * B] + products[:, 4 * B :]
    ll = products[:B, 2 * B : 3 * B]
    lr = products[:B, 3 * B : 4 * B]
    rl = products[B:, 2 * B : 3 * B]
    rr = products[B:, 3 * B : 4 * B]
    part[:B, :] = whole[:B, :B] + (ll + ll.T)
    part[B : 2 * B, :] = whole[:B, B:] + (lr + rl.T)
    part[2 * B :, :] = whole[B:, B:] + (rr + rr.T)


HALF = 3 * B // 2
SUM_SCRATCH = [
    pltpu.VMEM((HALF, B), F32),
    pltpu.VMEM((HALF, B), F32),
    pltpu.VMEM((HALF, B), F32),
    pltpu.VMEM((3 * B, B), F32),
    pltpu.SemaphoreType.DMA((3,)),
    pltpu.SemaphoreType.DMA((3,)),
]


def row_neighbours():
    pair, row = lax.axis_index("pair"), lax.axis_index("row")
    core, chip = lax.rem(row, 2), lax.div(row, 2)
    return core, (pair, 2 * chip + 1 - core), (pair, 2 * (1 - chip) + core)


def greet(devices):
    for device in devices:
        pl.semaphore_signal(pltpu.get_barrier_semaphore(), inc=1, device_id=device, device_id_type=MESH)


def remote(src, dst, send, recv, device):
    return pltpu.make_async_remote_copy(
        src_ref=src, dst_ref=dst, send_sem=send, recv_sem=recv, device_id=device, device_id_type=MESH
    )


def row_sum(part, recv_a, acc, recv_b, full, send, recv):
    core, mate, across = row_neighbours()
    mine, other = pl.ds(core * HALF, HALF), pl.ds((1 - core) * HALF, HALF)
    pl.semaphore_wait(pltpu.get_barrier_semaphore(), 2)
    first = remote(part.at[other, :], recv_a, send.at[0], recv.at[0], mate)
    first.start()
    first.wait()
    acc[...] = part[mine, :] + recv_a[...]
    second = remote(acc, recv_b, send.at[1], recv.at[1], across)
    second.start()
    second.wait()
    full[mine, :] = acc[...] + recv_b[...]
    third = remote(full.at[mine, :], full.at[mine, :], send.at[2], recv.at[2], mate)
    third.start()
    third.wait()


def round_kernel(count, *refs):
    ins, refs = refs[:count], refs[count:]
    left_out, right_out, x, v_high, v_low, load, store, part = refs[:8]
    gram, sums, solve = refs[8:9], refs[9:15], refs[15:]
    core, mate, across = row_neighbours()
    greet((mate, across))

    def loads(i):
        if count == 1:
            return [pltpu.make_async_copy(ins[0].at[chunk(i), :], x.at[chunk(i), :], load.at[i, 0])]
        return [
            pltpu.make_async_copy(ins[j].at[chunk(i), :], x.at[chunk(i), pl.ds(j * B, B)], load.at[i, j])
            for j in range(2)
        ]

    def stores(i):
        return [
            pltpu.make_async_copy(x.at[chunk(i), pl.ds(j * B, B)], out.at[chunk(i), :], store.at[i, j])
            for j, out in enumerate((left_out, right_out))
        ]

    @pl.loop(0, CHUNKS)
    def _(i):
        for c in loads(i):
            c.start()

    gram_clear(*gram)

    @pl.loop(0, CHUNKS)
    def _(i):
        for c in loads(i):
            c.wait()
        gram_add(x[chunk(i), :], *gram)

    gram_blocks(*gram, part)
    row_sum(part, *sums)
    full = sums[3]
    halves = jacobi(full[:B, :], full[B : 2 * B, :], full[2 * B :, :], solve[:4], *solve[4:])
    for j, half in enumerate(halves):
        v_high[:, j * B : (j + 1) * B], v_low[:, j * B : (j + 1) * B] = split(half)
    dot = functools.partial(jnp.dot, preferred_element_type=F32)

    @pl.loop(0, CHUNKS)
    def _(i):
        high, low = split(x[chunk(i), :])
        x[chunk(i), :] = dot(high, v_high[...]) + (dot(high, v_low[...]) + dot(low, v_high[...]))
        for c in stores(i):
            c.start()

    @pl.loop(0, CHUNKS)
    def _(i):
        for c in stores(i):
            c.wait()


def one_round(index, *ins):
    return pl.pallas_call(
        functools.partial(round_kernel, len(ins)),
        out_shape=(jax.ShapeDtypeStruct((ROWS, B), F32),) * 2,
        in_specs=[HBM] * len(ins),
        out_specs=(HBM, HBM),
        scratch_shapes=[
            pltpu.VMEM((ROWS, 2 * B), F32),
            pltpu.VMEM((2 * B, 2 * B), BF16),
            pltpu.VMEM((2 * B, 2 * B), BF16),
            pltpu.SemaphoreType.DMA((CHUNKS, 2)),
            pltpu.SemaphoreType.DMA((CHUNKS, 2)),
            pltpu.VMEM((3 * B, B), F32),
        ]
        + GRAM_SCRATCH
        + SUM_SCRATCH
        + JACOBI_SCRATCH,
        compiler_params=pltpu.CompilerParams(
            collective_id=index, has_side_effects=True, vmem_limit_bytes=VMEM_LIMITS[len(ins) - 1]
        ),
        cost_estimate=pl.CostEstimate(
            flops=10 * ROWS * (2 * B) ** 2, bytes_accessed=4 * ROWS * 2 * B * 2, transcendentals=0
        ),
        name="round",
    )(*ins)


LOW_BITS = 3
VMEM_LIMITS = (60 * 2**20, 40 * 2**20)


def transfer_kernel(mask, block, out, send, recv):
    to = (jnp.bitwise_xor(lax.axis_index("pair"), mask), lax.axis_index("row"))
    if transfer_id(mask) is not None:
        greet((to,))
        pl.semaphore_wait(pltpu.get_barrier_semaphore(), 1)
    copy = remote(block, out, send, recv, to)
    copy.start()
    copy.wait()


def transfer(mask, block):
    if mask == 0:
        return block
    return pl.pallas_call(
        functools.partial(transfer_kernel, mask),
        out_shape=jax.ShapeDtypeStruct(block.shape, block.dtype),
        in_specs=[HBM],
        out_specs=HBM,
        scratch_shapes=[pltpu.SemaphoreType.DMA, pltpu.SemaphoreType.DMA],
        compiler_params=pltpu.CompilerParams(collective_id=transfer_id(mask), has_side_effects=True),
        cost_estimate=pl.CostEstimate(flops=0, bytes_accessed=2 * ROWS * B * 4, transcendentals=0),
        name="transfer",
    )(block)


OWN_BARRIERS = 36


def transfer_id(mask):
    number = 3 if mask == lax.axis_size("pair") - 1 else mask + 3
    return number if number <= OWN_BARRIERS else None


def route(block, mask):
    count = lax.axis_size("pair")
    low_count = 1 << LOW_BITS

    def high_part(high, block):
        return lax.switch(
            jnp.bitwise_and(mask, low_count - 1),
            [functools.partial(transfer, high * low_count + low) for low in range(low_count)],
            block,
        )

    return lax.switch(
        jnp.right_shift(mask, LOW_BITS), [functools.partial(high_part, h) for h in range(count // low_count)], block
    )


def local(matrix, plan):
    left, right = one_round(1, matrix)
    right = route(right, plan[0])
    left, right = one_round(2, left, right)
    return jnp.concatenate([left, route(right, plan[1])], axis=1)


def solution(mesh):
    return jax.shard_map(
        local, mesh=mesh, in_specs=(P("row", "pair"), P()), out_specs=P("row", "pair"), check_vma=False
    )
```

```python
import functools
import jax
import jax.numpy as jnp
from jax import lax
from jax.experimental import pallas as pl
from jax.experimental.pallas import tpu as pltpu
from jax.sharding import PartitionSpec as P

F32 = jnp.float32
BF16 = jnp.bfloat16
B = 128
SETS = 16


def lanes(shape):
    return lax.broadcasted_iota(jnp.int32, shape, len(shape) - 1)


def lane_gather(x, index):
    return jnp.take_along_axis(x, jnp.broadcast_to(index, x.shape), axis=1, mode="promise_in_bounds")


def shift_lanes(top, bottom):
    lane = lanes(top.shape)
    new_top = jnp.where(lane == B - 1, bottom, pltpu.roll(top, B - 1, 1))
    new_bottom = jnp.where(lane == 0, bottom, pltpu.roll(jnp.where(lane == 0, top, bottom), 1, 1))
    return new_top, new_bottom


def angles(first, second, coupling, step):
    lane = lanes(first.shape)
    top_is_lower = (lane == 0) | (lane > step)
    difference = second - first
    forward = (difference > 0) | ((difference == 0) & top_is_lower)
    tangent = jnp.where(forward, 2.0, -2.0) * coupling / (
        jnp.abs(difference)
        + jnp.sqrt(difference * difference + 4.0 * coupling * coupling)
        + 1e-06 * (first + second)
    )
    square = 1.0 + tangent * tangent
    cosine = 1.0 / jnp.sqrt(square)
    cosine += 0.5 * cosine * (1.0 - square * cosine * cosine)
    return cosine, cosine * tangent


def one_set(step, p, grams, v_top, v_bot):
    tt, tb, bt, bb = grams
    q = 1 - p
    eye = lax.broadcasted_iota(jnp.int32, (B, B), 0) == lanes((B, B))
    diag = lambda ref, base: jnp.sum(jnp.where(eye, ref[p, base : base + B, :], 0.0), axis=0, keepdims=True)
    cosine, sine = angles(diag(tt, 1), diag(bb, 7), diag(tb, 1), step)
    col_c = jnp.broadcast_to(cosine, (B, B)).T
    col_s = jnp.broadcast_to(sine, (B, B)).T
    n = 32
    for k in range(0, B, n):
        a, b = tt[p, 1 + k : 1 + k + n, :], tb[p, 1 + k : 1 + k + n, :]
        c, d = bt[p, 7 + k : 7 + k + n, :], bb[p, 7 + k : 7 + k + n, :]
        a, b = cosine * a - sine * b, cosine * b + sine * a
        c, d = cosine * c - sine * d, cosine * d + sine * c
        cc, ss = col_c[k : k + n], col_s[k : k + n]
        a, c = cc * a - ss * c, cc * c + ss * a
        b, d = cc * b - ss * d, cc * d + ss * b
        a, b = shift_lanes(a, b)
        c, d = shift_lanes(c, d)
        tt[q, k : k + n, :], tb[q, k : k + n, :] = a, b
        bt[q, 8 + k : 8 + k + n, :], bb[q, 8 + k : 8 + k + n, :] = c, d
    for top, bottom in ((tt, bt), (tb, bb)):
        first = bottom[q, 8:9, :]
        top[q, B : B + 1, :] = bottom[q, B + 7 : B + 8, :]
        bottom[q, 7:8, :] = first
        bottom[q, 8:9, :] = top[q, 0:1, :]
    for k in range(0, 2 * B, n):
        a, b = v_top[k : k + n, :], v_bot[k : k + n, :]
        a, b = shift_lanes(cosine * a - sine * b, cosine * b + sine * a)
        v_top[k : k + n, :], v_bot[k : k + n, :] = a, b


def jacobi(ll, lr, rr, grams, v_top, v_bot):
    tt, tb, bt, bb = grams
    lane = lanes((1, B))
    lr = lane_gather(lr, B - 1 - lane)
    rr = lane_gather(lane_gather(rr, B - 1 - lane).T, B - 1 - lane)
    tt[0, 1 : B + 1, :] = ll
    tb[0, 1 : B + 1, :] = lr
    bt[0, 7 : B + 7, :] = lr.T
    bb[0, 7 : B + 7, :] = rr
    row = lax.broadcasted_iota(jnp.int32, (2 * B, B), 0)
    v_top[...] = jnp.where(row == lanes((2 * B, B)), 1.0, 0.0)
    v_bot[...] = jnp.where(row + lanes((2 * B, B)) == 2 * B - 1, 1.0, 0.0)

    @pl.loop(0, SETS // 2)
    def _(i):
        one_set(2 * i, 0, grams, v_top, v_bot)
        one_set(2 * i + 1, 1, grams, v_top, v_bot)

    top, bottom = v_top[...], v_bot[...]
    lane = lanes((1, B))
    moved = pltpu.roll(top, SETS, 1)
    low = lane < SETS
    left = jnp.where(low, lane_gather(bottom, (SETS - lane) & (B - 1)), moved)
    right = jnp.where(low, moved, lane_gather(bottom, jnp.where(lane == B - 1, 0, (B + SETS - 1 - lane) & (B - 1))))
    return left, right


JACOBI_SCRATCH = [pltpu.VMEM((2, B + 16, B), F32) for _ in range(4)] + [pltpu.VMEM((2 * B, B), F32) for _ in range(2)]

ROWS = 4096
CHUNK = 512
CHUNKS = ROWS // CHUNK
MESH = pl.DeviceIdType.MESH
HBM = pl.BlockSpec(memory_space=pl.ANY)
WHOLE = pl.BlockSpec(memory_space=pltpu.VMEM)


def chunk(i):
    return pl.ds(pl.multiple_of(i * CHUNK, CHUNK), CHUNK)


def split(x):
    high = x.astype(BF16)
    return high, (x - high.astype(F32)).astype(BF16)


GRAM_SCRATCH = [pltpu.VMEM((2 * B, 6 * B), F32)]


def gram_clear(products):
    products[...] = jnp.zeros_like(products)


def gram_add(x, products):
    high = x.astype(BF16)
    rest = x - high.astype(F32)
    middle, low = split(rest)
    product = functools.partial(
        lax.dot_general, dimension_numbers=(((0,), (0,)), ((), ())), preferred_element_type=F32
    )
    products[:, : 4 * B] += product(high, jnp.concatenate([high, middle], axis=1))
    products[:, 2 * B : 4 * B] += product(high, low)
    products[:, 4 * B :] += product(middle, middle)


def gram_blocks(products, part):
    whole = products[:, : 2 * B] + products[:, 4 * B :]
    ll = products[:B, 2 * B : 3 * B]
    lr = products[:B, 3 * B : 4 * B]
    rl = products[B:, 2 * B : 3 * B]
    rr = products[B:, 3 * B : 4 * B]
    part[:B, :] = whole[:B, :B] + (ll + ll.T)
    part[B : 2 * B, :] = whole[:B, B:] + (lr + rl.T)
    part[2 * B :, :] = whole[B:, B:] + (rr + rr.T)


HALF = 3 * B // 2
SUM_SCRATCH = [
    pltpu.VMEM((HALF, B), F32),
    pltpu.VMEM((HALF, B), F32),
    pltpu.VMEM((HALF, B), F32),
    pltpu.VMEM((3 * B, B), F32),
    pltpu.SemaphoreType.DMA((3,)),
    pltpu.SemaphoreType.DMA((3,)),
]


def row_neighbours():
    pair, row = lax.axis_index("pair"), lax.axis_index("row")
    core, chip = lax.rem(row, 2), lax.div(row, 2)
    return core, (pair, 2 * chip + 1 - core), (pair, 2 * (1 - chip) + core)


def greet(devices):
    for device in devices:
        pl.semaphore_signal(pltpu.get_barrier_semaphore(), inc=1, device_id=device, device_id_type=MESH)


def remote(src, dst, send, recv, device):
    return pltpu.make_async_remote_copy(
        src_ref=src, dst_ref=dst, send_sem=send, recv_sem=recv, device_id=device, device_id_type=MESH
    )


def row_sum(part, recv_a, acc, recv_b, full, send, recv):
    core, mate, across = row_neighbours()
    mine, other = pl.ds(core * HALF, HALF), pl.ds((1 - core) * HALF, HALF)
    pl.semaphore_wait(pltpu.get_barrier_semaphore(), 2)
    first = remote(part.at[other, :], recv_a, send.at[0], recv.at[0], mate)
    first.start()
    first.wait()
    acc[...] = part[mine, :] + recv_a[...]
    second = remote(acc, recv_b, send.at[1], recv.at[1], across)
    second.start()
    second.wait()
    full[mine, :] = acc[...] + recv_b[...]
    third = remote(full.at[mine, :], full.at[mine, :], send.at[2], recv.at[2], mate)
    third.start()
    third.wait()


def round_kernel(count, *refs):
    ins, refs = refs[:count], refs[count:]
    left_out, right_out, x, v_high, v_middle, v_low, load, store, part = refs[:9]
    gram, sums, solve = refs[9:10], refs[10:16], refs[16:]
    core, mate, across = row_neighbours()
    greet((mate, across))

    def loads(i):
        if count == 1:
            return [pltpu.make_async_copy(ins[0].at[chunk(i), :], x.at[chunk(i), :], load.at[i, 0])]
        return [
            pltpu.make_async_copy(ins[j].at[chunk(i), :], x.at[chunk(i), pl.ds(j * B, B)], load.at[i, j])
            for j in range(2)
        ]

    def stores(i):
        return [
            pltpu.make_async_copy(x.at[chunk(i), pl.ds(j * B, B)], out.at[chunk(i), :], store.at[i, j])
            for j, out in enumerate((left_out, right_out))
        ]

    @pl.loop(0, CHUNKS)
    def _(i):
        for c in loads(i):
            c.start()

    gram_clear(*gram)

    @pl.loop(0, CHUNKS)
    def _(i):
        for c in loads(i):
            c.wait()
        gram_add(x[chunk(i), :], *gram)

    gram_blocks(*gram, part)
    row_sum(part, *sums)
    full = sums[3]
    halves = jacobi(full[:B, :], full[B : 2 * B, :], full[2 * B :, :], solve[:4], *solve[4:])
    for j, half in enumerate(halves):
        columns = slice(j * B, (j + 1) * B)
        high = half.astype(BF16)
        v_high[:, columns] = high
        v_middle[:, columns], v_low[:, columns] = split(half - high.astype(F32))
    dot = functools.partial(jnp.dot, preferred_element_type=F32)

    @pl.loop(0, CHUNKS)
    def _(i):
        high, low = split(x[chunk(i), :])
        x[chunk(i), :] = dot(high, v_high[...]) + (
            dot(high, v_middle[...]) + (dot(low, v_high[...]) + dot(high, v_low[...]))
        )
        for c in stores(i):
            c.start()

    @pl.loop(0, CHUNKS)
    def _(i):
        for c in stores(i):
            c.wait()


def one_round(index, *ins):
    return pl.pallas_call(
        functools.partial(round_kernel, len(ins)),
        out_shape=(jax.ShapeDtypeStruct((ROWS, B), F32),) * 2,
        in_specs=[HBM] * len(ins),
        out_specs=(HBM, HBM),
        scratch_shapes=[
            pltpu.VMEM((ROWS, 2 * B), F32),
            pltpu.VMEM((2 * B, 2 * B), BF16),
            pltpu.VMEM((2 * B, 2 * B), BF16),
            pltpu.VMEM((2 * B, 2 * B), BF16),
            pltpu.SemaphoreType.DMA((CHUNKS, 2)),
            pltpu.SemaphoreType.DMA((CHUNKS, 2)),
            pltpu.VMEM((3 * B, B), F32),
        ]
        + GRAM_SCRATCH
        + SUM_SCRATCH
        + JACOBI_SCRATCH,
        compiler_params=pltpu.CompilerParams(
            collective_id=index, has_side_effects=True, vmem_limit_bytes=VMEM_LIMIT
        ),
        cost_estimate=pl.CostEstimate(
            flops=10 * ROWS * (2 * B) ** 2, bytes_accessed=4 * ROWS * 2 * B * 2, transcendentals=0
        ),
        name="round",
    )(*ins)


LOW_BITS = 3
VMEM_LIMIT = 60 * 2**20


def transfer_kernel(mask, block, out, send, recv):
    to = (jnp.bitwise_xor(lax.axis_index("pair"), mask), lax.axis_index("row"))
    if transfer_id(mask) is not None:
        greet((to,))
        pl.semaphore_wait(pltpu.get_barrier_semaphore(), 1)
    copy = remote(block, out, send, recv, to)
    copy.start()
    copy.wait()


def transfer(mask, block):
    if mask == 0:
        return block
    return pl.pallas_call(
        functools.partial(transfer_kernel, mask),
        out_shape=jax.ShapeDtypeStruct(block.shape, block.dtype),
        in_specs=[HBM],
        out_specs=HBM,
        scratch_shapes=[pltpu.SemaphoreType.DMA, pltpu.SemaphoreType.DMA],
        compiler_params=pltpu.CompilerParams(collective_id=transfer_id(mask), has_side_effects=True),
        cost_estimate=pl.CostEstimate(flops=0, bytes_accessed=2 * ROWS * B * 4, transcendentals=0),
        name="transfer",
    )(block)


OWN_BARRIERS = 36


def transfer_id(mask):
    number = 3 if mask == lax.axis_size("pair") - 1 else mask + 3
    return number if number <= OWN_BARRIERS else None


def route(block, mask):
    count = lax.axis_size("pair")
    low_count = 1 << LOW_BITS

    def high_part(high, block):
        return lax.switch(
            jnp.bitwise_and(mask, low_count - 1),
            [functools.partial(transfer, high * low_count + low) for low in range(low_count)],
            block,
        )

    return lax.switch(
        jnp.right_shift(mask, LOW_BITS), [functools.partial(high_part, h) for h in range(count // low_count)], block
    )


def local(matrix, plan):
    left, right = one_round(1, matrix)
    right = route(right, plan[0])
    left, right = one_round(2, left, right)
    return jnp.concatenate([left, route(right, plan[1])], axis=1)


def solution(mesh):
    return jax.shard_map(
        local, mesh=mesh, in_specs=(P("row", "pair"), P()), out_specs=P("row", "pair"), check_vma=False
    )
```
